32 devices in a mesh: job: 2 (over y), tok: 4 (over z), can: 4 (over x, core).
Axes of the slice: x: 2, y: 2, z: 4, core: 2. Of those that a mesh axis runs over, the one named last changes fastest.
Arguments:
- train_acts: bfloat16 [4096, 14336], P(('job', 'tok')), parts along dimension 0, may hold values from -6 to 6
- train_grads: bfloat16 [4096, 4096], P(('job', 'tok')), parts along dimension 0, may hold values from -6 to 6
- train_segment: int32 [4096], P(('job', 'tok')), parts along dimension 0, may hold values from 0 to 15, as said below
- canary_acts: bfloat16 [1024, 14336], P(('job', 'tok', 'can')), parts along dimension 0, may hold values from -6 to 6
- canary_grads: bfloat16 [1024, 4096], P(('job', 'tok', 'can')), parts along dimension 0, may hold values from -6 to 6
- canary_segment: int32 [1024], P(('job', 'tok', 'can')), parts along dimension 0, may hold values from 0 to 15, never falling along the last dimension, each value on 1 to 64 neighbouring positions
Outputs:
- scores: float32 [32, 16], P(('job', 'tok'), 'can'), parts along dimension 0
The draws below stay inside these ranges and needn't reach their ends.
There are 2 independent parts, one for each index of `job`. The reference program is written for one: setup_inputs(seed, part) draws one part's arguments, and reference() takes and returns one part's arrays. A program takes and returns all parts, laid end to end along the dimension named above; each array names one. Nothing has to cross between parts.
Inputs may be any that keep to these rules, and one draw needn't show every extreme that they name: `train_segment`: ids never fall; the 512 training tokens of block b (tokens b * 512 to b * 512 + 511) belong to the sequences b * 4 to b * 4 + 3, each of them non-empty. `canary_segment`: ids never fall; every canary sequence has 1 to 64 tokens.
All inputs are finite; a program needn't handle non-finite values.
Results may differ from the reference program's by a relative error of at most 0.0003.
Values may be sent and summed in bfloat16 or wider, within the bound.
No kernel may reach another device: no remote copies, remote signals or barrier semaphores. Data moves between devices by JAX's collectives and lax.ppermute only.
A program may use at most 64 MiB of HBM per device.

```python
import math
import jax
import jax.numpy as jnp
import numpy as np
from jax import lax

FF = 14336
D = 4096
TOK_DEV = 512
SEQ_DEV = 4
CSEQ = 16
TOKENS = 2048
TSEQ = 16
CANARY = 512
N_TOK = 4


def draw_train_segment(key, part):
    key = jax.random.fold_in(key, 11)
    blocks = TOKENS // TOK_DEV
    block_keys = jax.random.split(key, blocks)

    def segment_block(block_key):
        boundaries = jax.random.permutation(block_key, TOK_DEV - 1)[:SEQ_DEV - 1] + 1
        positions = jnp.arange(TOK_DEV, dtype=jnp.int32)
        return jnp.sum((positions[:, None] >= boundaries[None, :]).astype(jnp.int32), axis=1)
    local_ids = jax.vmap(segment_block)(block_keys)
    offsets = (jnp.arange(blocks, dtype=jnp.int32) * SEQ_DEV)[:, None]
    return (local_ids + offsets).reshape(TOKENS).astype(jnp.int32)


def steps_of(own_key, dims, cuts, smallest, largest):
    level = 1.0
    for axis_at, blocks in cuts:
        steps = jax.random.uniform(jax.random.fold_in(jax.random.fold_in(own_key, 6), axis_at), (blocks,), jnp.float32, smallest / len(cuts), largest / len(cuts))
        level = level * jnp.repeat(jnp.exp(steps), dims[axis_at] // blocks).reshape((-1,) + (1,) * (len(dims) - 1 - axis_at))
    return level


def length_profile(count, total, reach, lean):
    loads = [(1 << 20) // math.isqrt(standing ** lean) + 1 for standing in range(2, count + 1)]
    rest, counts = total - reach - (count - 1), [1] * (count - 1)
    while rest > 0:
        candidates = [i for i in range(count - 1) if counts[i] < reach]
        whole, remaining = sum([loads[i] for i in candidates]), rest
        for i in candidates:
            addition = min(reach - counts[i], max(1, remaining * loads[i] // whole), rest)
            counts[i] = counts[i] + addition
            rest = rest - addition
    return np.array([reach] + counts)


def ragged_sizes(key, count, total, reach, lean):
    if count == 2:
        one = jax.random.randint(key, (), max(1, total - reach), min(reach, total - 1) + 1)
        return jnp.stack([one, total - one])
    tallies = jnp.asarray(length_profile(count, total, reach, lean), jnp.int32)
    couples = (count - 1) // 2
    donor, taker = tallies[1:1 + 2 * couples:2], tallies[2:2 + 2 * couples:2]
    slack = jnp.minimum(donor - 1, reach - taker)
    moved = jax.random.randint(jax.random.fold_in(key, 1), (couples,), 0, 1 << 20) % (slack + 1)
    tallies = tallies.at[1:1 + 2 * couples:2].set(donor - moved).at[2:2 + 2 * couples:2].set(taker + moved)
    return tallies[jax.random.permutation(jax.random.fold_in(key, 2), count)]


def noise(rng, shape, width, bound, shards=(), held_as=jnp.bfloat16):
    values = jax.random.normal(rng, shape, jnp.float32) * width
    if len(shards) > 0:
        values = steps_of(rng, shape, shards, -0.22, 0.18) * values
    return jnp.clip(values, min=-bound, max=bound).astype(held_as)


def setup_inputs(seed: int = 0, part: int = 0) -> dict:
    key_list = jax.random.split(jax.random.key(seed), 7)
    part_splits = jax.random.split(jax.random.fold_in(key_list[6], part), 7)
    return {
        "train_acts": noise(part_splits[0], (TOKENS, FF), 1.0, 6.0, ((0, 4),)),
        "train_grads": noise(part_splits[1], (TOKENS, D), 1.0, 6.0, ((0, 4),)),
        "train_segment": draw_train_segment(jax.random.fold_in(jax.random.fold_in(key_list[6], part), 71), part),
        "canary_acts": noise(part_splits[3], (CANARY, FF), 1.0, 6.0, ((0, 16),)),
        "canary_grads": noise(part_splits[4], (CANARY, D), 1.0, 6.0, ((0, 16),)),
        "canary_segment": jnp.searchsorted(jnp.cumsum(ragged_sizes(part_splits[5], CSEQ, CANARY, 2 * CANARY // CSEQ, 1)), jnp.arange(CANARY), side="right").astype(jnp.int32),
    }


def reference(train_acts, train_grads, train_segment, canary_acts, canary_grads, canary_segment):
    member = (canary_segment[:, None] == jnp.arange(CSEQ, dtype=jnp.int32)[None, :]).astype(jnp.float32)
    contract = (((1,), (1,)), ((), ()))

    def block_terms(index):
        start = (index * TOK_DEV).astype(jnp.int32)
        acts_block = lax.dynamic_slice_in_dim(train_acts, start, TOK_DEV, 0)
        grads_block = lax.dynamic_slice_in_dim(train_grads, start, TOK_DEV, 0)
        seg_block = lax.dynamic_slice_in_dim(train_segment, start, TOK_DEV, 0)
        x_gram = lax.dot_general(acts_block, canary_acts, contract, preferred_element_type=jnp.float32)
        g_gram = lax.dot_general(grads_block, canary_grads, contract, preferred_element_type=jnp.float32)
        per_token = jnp.dot(x_gram * g_gram, member, precision=lax.Precision.HIGHEST, preferred_element_type=jnp.float32)
        self_x = lax.dot_general(acts_block, acts_block, contract, preferred_element_type=jnp.float32)
        self_g = lax.dot_general(grads_block, grads_block, contract, preferred_element_type=jnp.float32)
        local_ids = seg_block - index * SEQ_DEV
        owner = (local_ids[:, None] == jnp.arange(SEQ_DEV, dtype=jnp.int32)[None, :]).astype(jnp.float32)
        left = jnp.dot(self_x * self_g, owner, precision=lax.Precision.HIGHEST, preferred_element_type=jnp.float32)
        self_score = lax.optimization_barrier(jnp.sum(owner * left, axis=0))
        return (per_token, self_score)
    per_token, self_score = lax.map(block_terms, jnp.arange(N_TOK, dtype=jnp.int32))
    per_token = per_token.reshape(TOKENS, CSEQ)
    self_score = self_score.reshape(TSEQ)
    raw = jax.ops.segment_sum(per_token, train_segment, num_segments=TSEQ)
    scale = math.sqrt(FF * D * (CANARY / CSEQ))
    norm_factor = jnp.sqrt(self_score / (FF * D) + 1.0)
    return raw / (scale * norm_factor[:, None])
```

```python
import math

import jax
import jax.numpy as jnp
from jax import lax
from jax.experimental import pallas as pl
from jax.experimental.pallas import tpu as pltpu
from jax.sharding import PartitionSpec as P

FF = 14336
D = 4096
SEQ_DEV = 4
CSEQ = 16
LANES = 128
FIRST = 10752
ROWS = (((1,), (1,)), ((), ()))


def gram(left, right):
    return lax.dot_general(left, right, ROWS, preferred_element_type=jnp.float32)


def exact(left, right, dims):
    return lax.dot_general(
        left, right, (dims, ((), ())), precision=lax.Precision.HIGHEST, preferred_element_type=jnp.float32
    )


def after(value, *earlier):
    return lax.optimization_barrier((value,) + earlier)[0]


def after2(one, two, earlier):
    return lax.optimization_barrier((one, two) + tuple(earlier))[:2]


def call(kernel, scalar, inputs, specs, steps, out, scratch, depth, name):
    return pl.pallas_call(
        kernel,
        grid_spec=pltpu.PrefetchScalarGridSpec(
            num_scalar_prefetch=1,
            grid=(steps,),
            in_specs=specs,
            out_specs=pl.BlockSpec(out, lambda k, s: (0, 0)),
            scratch_shapes=scratch,
        ),
        out_shape=jax.ShapeDtypeStruct(out, jnp.float32),
        cost_estimate=pl.CostEstimate(flops=512 * 256 * depth, bytes_accessed=1024 * depth, transcendentals=0),
        compiler_params=pltpu.CompilerParams(vmem_limit_bytes=56 << 20),
        name=name,
    )(scalar.reshape(1).astype(jnp.int32), *inputs)


def in_order(z, own, down, up, second, far):
    return jnp.concatenate([own, jnp.where(z < 3, down, far), second, jnp.where(z > 0, up, far)], axis=0)


def cross_gram(base, train, pieces, cut, block):
    rows, per = train.shape[0], pieces[0].shape[0]
    low, high = cut

    def kernel(z_ref, base_ref, train_ref, own, down, up, second, far, out_ref):
        right = in_order(z_ref[0], own[...], down[...], up[...], second[...], far[...])
        part = gram(train_ref[...], right)

        @pl.when(pl.program_id(0) == 0)
        def _():
            out_ref[...] = base_ref[...] + part

        @pl.when(pl.program_id(0) > 0)
        def _():
            out_ref[...] += part

    whole = pl.BlockSpec((rows, 4 * per), lambda k, s: (0, 0))
    near = pl.BlockSpec((per, block), lambda k, s: (0, low // block + k))
    late = pl.BlockSpec((per, block), lambda k, s: (0, k))
    wide = pl.BlockSpec((rows, block), lambda k, s: (0, low // block + k))
    specs = [whole, wide] + [near] * 3 + [late] * 2
    inputs = (base, train) + tuple(pieces)
    steps = (high - low) // block
    return call(kernel, lax.axis_index("tok"), inputs, specs, steps, (rows, 4 * per), [], high - low, "cross_gram")


def score_shares(x_gram, owner_rows, self_rows, train, pieces, block):
    rows, depth = train.shape
    per = pieces[0].shape[0]
    steps = depth // block

    def kernel(z_ref, x_ref, owner_ref, self_ref, train_ref, *refs):
        total, out_ref = refs[-1], refs[-2]
        z = z_ref[0]
        part = gram(train_ref[...], in_order(z, *[r[...] for r in refs[:5]]))

        @pl.when(pl.program_id(0) == 0)
        def _():
            total[...] = part

        @pl.when(pl.program_id(0) > 0)
        def _():
            total[...] += part

        @pl.when(pl.program_id(0) == steps - 1)
        def _():
            pair = x_ref[...] * total[...]
            by_train = exact(owner_ref[...], pair, ((1,), (0,)))
            ids = in_order(z, *[r[...].astype(jnp.float32) for r in refs[5:10]])
            lane = lax.broadcasted_iota(jnp.int32, ids.shape, 1)
            member = (ids == lane.astype(jnp.float32)).astype(jnp.float32)
            scores = exact(by_train, member, ((1,), (0,)))
            out_ref[...] = jnp.where(lax.broadcasted_iota(jnp.int32, scores.shape, 1) < CSEQ, scores, self_ref[...])

    whole = pl.BlockSpec((rows, 4 * per), lambda k, s: (0, 0))
    wide = pl.BlockSpec((rows, block), lambda k, s: (0, k))
    piece = pl.BlockSpec((per, block), lambda k, s: (0, k))
    tag = pl.BlockSpec((per, LANES), lambda k, s: (0, depth // LANES))
    seq = owner_rows.shape[0]
    specs = [
        whole,
        pl.BlockSpec((seq, rows), lambda k, s: (0, 0)),
        pl.BlockSpec((seq, LANES), lambda k, s: (0, 0)),
        wide,
    ]
    specs = specs + [piece] * 5 + [tag] * 5
    inputs = (x_gram, owner_rows, self_rows, train) + tuple(pieces) * 2
    scratch = [pltpu.VMEM((rows, 4 * per), jnp.float32)]
    return call(kernel, lax.axis_index("tok"), inputs, specs, steps, (seq, LANES), scratch, depth, "score_shares")


DOWN = [(1, 0), (2, 1), (3, 2)]
UP = [(0, 1), (1, 2), (2, 3)]
FAR = [(1, 0), (2, 3)]


def line_scores(train_acts, train_grads, owner_rows, self_rows, canary_acts, canary_grads, canary_segment):
    z = lax.axis_index("tok")
    tag = jnp.broadcast_to(canary_segment.astype(canary_grads.dtype)[:, None], (canary_segment.shape[0], LANES))
    tagged = jnp.concatenate([canary_grads, tag], axis=1)

    acts_down = lax.ppermute(canary_acts, "tok", DOWN)
    acts_up = lax.ppermute(canary_acts, "tok", UP)
    grads_down = lax.ppermute(tagged, "tok", DOWN)
    grads_up = lax.ppermute(tagged, "tok", UP)

    acts_down, acts_up = after2(acts_down, acts_up, ())
    acts_down2 = lax.ppermute(acts_down, "tok", DOWN[:2])
    acts_up2 = lax.ppermute(acts_up, "tok", UP[1:])
    grads_down, grads_up = after2(grads_down, grads_up, (acts_down, acts_up))
    grads_down2 = lax.ppermute(grads_down, "tok", DOWN[:2])
    grads_up2 = lax.ppermute(grads_up, "tok", UP[1:])

    acts_down2, acts_up2 = after2(acts_down2, acts_up2, (grads_down, grads_up))
    second_a = jnp.where(z < 2, acts_down2[:, :FIRST], acts_up2[:, :FIRST])
    far_a = lax.ppermute(second_a, "tok", FAR)
    acts_down2, acts_up2 = after2(acts_down2, acts_up2, (second_a,))
    second_b = jnp.where(z < 2, acts_down2[:, FIRST:], acts_up2[:, FIRST:])
    far_b = lax.ppermute(second_b, "tok", FAR)
    grads_down2, grads_up2 = after2(grads_down2, grads_up2, (second_b,))
    second_g = jnp.where(z < 2, grads_down2, grads_up2)
    far_g = lax.ppermute(second_g, "tok", FAR)

    x_gram = jnp.zeros((train_acts.shape[0], 4 * canary_acts.shape[0]), jnp.float32)
    near = (canary_acts, acts_down, acts_up)
    x_gram = cross_gram(x_gram, train_acts, near + (second_a, far_a), (0, FIRST), 3584)
    x_gram = cross_gram(x_gram, train_acts, near + (second_b, after(far_b, x_gram)), (FIRST, FF), 1792)
    pieces = (tagged, grads_down, grads_up, second_g, after(far_g, x_gram))
    return score_shares(x_gram, owner_rows, self_rows, train_grads, pieces, 2048)


def finish(shares, canary_total):
    can = lax.axis_size("can")
    width = CSEQ // can
    total = shares
    for k in range(1, can):
        total = total + lax.ppermute(shares, "can", [(i, (i + k) % can) for i in range(can)])
    own = lax.dynamic_slice(total, (0, lax.axis_index("can") * width), (SEQ_DEV, width))
    scale = math.sqrt(FF * D * (canary_total / CSEQ))
    return own / (scale * jnp.sqrt(total[:SEQ_DEV, CSEQ] / (FF * D) + 1.0)[:, None])


def local(train_acts, train_grads, train_segment, canary_acts, canary_grads, canary_segment):
    tok, can = lax.axis_size("tok"), lax.axis_size("can")
    rows = train_acts.shape[0]
    canary_total = canary_acts.shape[0] * tok * can
    local_ids = train_segment - lax.axis_index("tok") * SEQ_DEV
    owner_rows = (jnp.arange(8, dtype=jnp.int32)[:, None] == local_ids[None, :]).astype(jnp.float32)

    share = rows // can
    start = lax.axis_index("can") * share
    self_pair = gram(train_acts, lax.dynamic_slice_in_dim(train_acts, start, share, 0))
    self_pair = self_pair * gram(train_grads, lax.dynamic_slice_in_dim(train_grads, start, share, 0))
    left = exact(owner_rows, self_pair, ((1,), (0,)))
    self_share = jnp.sum(left * lax.dynamic_slice_in_dim(owner_rows, start, share, 1), axis=1)
    self_rows = jnp.broadcast_to(self_share[:, None], (8, LANES))

    if tok == 4:
        shares = line_scores(
            train_acts, train_grads, owner_rows, self_rows, canary_acts, canary_grads, canary_segment
        )
    else:
        ids = lax.all_gather(canary_segment, "tok", axis=0, tiled=True)
        pair = gram(train_acts, lax.all_gather(canary_acts, "tok", axis=0, tiled=True))
        pair = pair * gram(train_grads, lax.all_gather(canary_grads, "tok", axis=0, tiled=True))
        member = (ids[:, None] == jnp.arange(CSEQ, dtype=jnp.int32)[None, :]).astype(jnp.float32)
        scores = exact(exact(owner_rows, pair, ((1,), (0,))), member, ((1,), (0,)))
        shares = jnp.concatenate([scores, self_rows[:, CSEQ:]], axis=1)
    return finish(shares, canary_total)


def solution(mesh):
    placed = (
        P(("job", "tok"), None),
        P(("job", "tok"), None),
        P(("job", "tok")),
        P(("job", "tok", "can"), None),
        P(("job", "tok", "can"), None),
        P(("job", "tok", "can")),
    )
    return jax.shard_map(
        local, mesh=mesh, in_specs=placed, out_specs=P(("job", "tok"), "can"), check_vma=False
    )
```

```python
import math

import jax
import jax.numpy as jnp
from jax import lax
from jax.experimental import pallas as pl
from jax.experimental.pallas import tpu as pltpu
from jax.sharding import PartitionSpec as P

FF = 14336
D = 4096
SEQ_DEV = 4
CSEQ = 16
LANES = 128
CUT = 10240
BLOCK = 2048
ROWS = (((1,), (1,)), ((), ()))


def gram(left, right):
    return lax.dot_general(left, right, ROWS, preferred_element_type=jnp.float32)


def exact(left, right, dims):
    return lax.dot_general(
        left, right, (dims, ((), ())), precision=lax.Precision.HIGHEST, preferred_element_type=jnp.float32
    )


def after(value, *earlier):
    return lax.optimization_barrier((value,) + earlier)[0]


def after2(one, two, earlier):
    return lax.optimization_barrier((one, two) + tuple(earlier))[:2]


def call(kernel, scalar, inputs, specs, steps, out, scratch, depth, name):
    return pl.pallas_call(
        kernel,
        grid_spec=pltpu.PrefetchScalarGridSpec(
            num_scalar_prefetch=1,
            grid=(steps,),
            in_specs=specs,
            out_specs=pl.BlockSpec(out, lambda k, s: (0, 0)),
            scratch_shapes=scratch,
        ),
        out_shape=jax.ShapeDtypeStruct(out, jnp.float32),
        cost_estimate=pl.CostEstimate(flops=512 * 256 * depth, bytes_accessed=1024 * depth, transcendentals=0),
        compiler_params=pltpu.CompilerParams(vmem_limit_bytes=60 << 20),
        name=name,
    )(scalar.reshape(1).astype(jnp.int32), *inputs)


def in_order(inner, own, first, middle, middle2, outer, outer2):
    return jnp.concatenate([own, first, jnp.where(inner, middle, outer), jnp.where(inner, middle2, outer2)], axis=0)


def cross_gram(base, train, low, place, pieces, first, count):
    rows, per = train.shape[0], pieces[0].shape[0]

    def kernel(place_ref, *refs):
        train_ref, out_ref = refs[-8], refs[-1]
        part = gram(train_ref[...], in_order(place_ref[0] == 1, *[r[...] for r in refs[-7:-1]]))

        @pl.when(pl.program_id(0) == 0)
        def _():
            out_ref[...] = part if base is None else refs[0][...] + part

        @pl.when(pl.program_id(0) > 0)
        def _():
            out_ref[...] += part

    specs = gram_specs(rows, per, low, first)
    inputs = (train,) + tuple(pieces)
    if base is not None:
        specs = [pl.BlockSpec((rows, 4 * per), lambda k, s: (0, 0))] + specs
        inputs = (base,) + inputs
    return call(kernel, place, inputs, specs, count, (rows, 4 * per), [], count * BLOCK, "cross_gram")


def gram_specs(rows, per, low, first):
    near = pl.BlockSpec((per, BLOCK), lambda k, s: (0, first + k))
    late = pl.BlockSpec((per, BLOCK), lambda k, s: (0, k))
    return [pl.BlockSpec((rows, BLOCK), lambda k, s: (0, low // BLOCK + k))] + [near] * 5 + [late]


def score_shares(x_gram, g_gram, owner_rows, self_terms, train, low, place, pieces, first, count, tags):
    rows, per = train.shape[0], pieces[0].shape[0]

    def kernel(place_ref, x_ref, g_ref, owner_ref, self_ref, *refs):
        inner, out_ref, total = place_ref[0] == 1, refs[-2], refs[-1]
        part = gram(refs[0][...], in_order(inner, *[r[...] for r in refs[1:7]]))

        @pl.when(pl.program_id(0) == 0)
        def _():
            total[...] = x_ref[...] + part

        @pl.when(pl.program_id(0) > 0)
        def _():
            total[...] += part

        @pl.when(pl.program_id(0) == count - 1)
        def _():
            by_train = exact(owner_ref[...], total[...] * g_ref[...], ((1,), (0,)))
            ids = in_order(inner, *[r[...].astype(jnp.float32) for r in refs[7:13]])
            lane = lax.broadcasted_iota(jnp.int32, ids.shape, 1)
            scores = exact(by_train, (ids == lane.astype(jnp.float32)).astype(jnp.float32), ((1,), (0,)))
            own = jnp.sum(self_ref[...], axis=1, keepdims=True)
            out_ref[...] = jnp.where(lax.broadcasted_iota(jnp.int32, scores.shape, 1) < CSEQ, scores, own)

    whole = pl.BlockSpec((rows, 4 * per), lambda k, s: (0, 0))
    seq = owner_rows.shape[0]
    specs = [
        whole,
        whole,
        pl.BlockSpec((seq, rows), lambda k, s: (0, 0)),
        pl.BlockSpec(self_terms.shape, lambda k, s: (0, 0)),
    ]
    specs = specs + gram_specs(rows, per, low, first)
    specs = specs + [pl.BlockSpec((per, LANES), lambda k, s, at=t.shape[1] // LANES - 1: (0, at)) for t in tags]
    inputs = (x_gram, g_gram, owner_rows, self_terms, train) + tuple(pieces) + tuple(tags)
    scratch = [pltpu.VMEM((rows, 4 * per), jnp.float32)]
    return call(kernel, place, inputs, specs, count, (seq, LANES), scratch, count * BLOCK, "score_shares")


SIDES = [(0, 1), (1, 0), (2, 3), (3, 2)]
MIDDLE = [(1, 2), (2, 1)]
OUTWARD = [(1, 0), (2, 3)]


def line_scores(train_acts, train_grads, owner_rows, self_terms, canary_acts, canary_grads, canary_segment):
    z = lax.axis_index("tok")
    place = jnp.where((z == 1) | (z == 2), 1, 0)
    tag = jnp.broadcast_to(canary_segment.astype(canary_grads.dtype)[:, None], (canary_segment.shape[0], LANES))
    x_own = canary_acts[:, :CUT]
    y_own = jnp.concatenate([canary_grads, canary_acts[:, CUT:], tag], axis=1)

    x_first = lax.ppermute(x_own, "tok", SIDES)
    x_middle = lax.ppermute(x_own, "tok", MIDDLE)
    y_first = lax.ppermute(y_own, "tok", SIDES)
    y_middle = lax.ppermute(y_own, "tok", MIDDLE)

    x_first, x_middle = after2(x_first, x_middle, ())
    x_middle2 = lax.ppermute(x_first, "tok", MIDDLE)
    x_outer = lax.ppermute(x_middle, "tok", OUTWARD)
    y_first, y_middle = after2(y_first, y_middle, (x_first, x_middle))
    y_middle2 = lax.ppermute(y_first, "tok", MIDDLE)
    y_outer = lax.ppermute(y_middle, "tok", OUTWARD)

    x_middle2, x_outer = after2(x_middle2, x_outer, (y_first, y_middle))
    far, last = [], ()
    for name, a, b in (("x", 0, 6144), ("x", 6144, CUT), ("y", 0, D), ("y", D, y_own.shape[1])):
        array = x_middle2 if name == "x" else y_middle2
        last = (after(array, *last)[:, a:b],)
        far.append(lax.ppermute(last[0], "tok", OUTWARD))
        if len(far) == 1:
            y_middle2, y_outer = after2(y_middle2, y_outer, last)
            last = (y_outer,)

    near = (x_own, x_first, x_middle, x_middle2, x_outer)
    x_gram = cross_gram(None, train_acts, 0, place, near + (far[0],), 0, 3)
    x_gram = cross_gram(x_gram, train_acts, 6144, place, near + (after(far[1], x_gram),), 3, 2)
    near = (y_own, y_first, y_middle, y_middle2, y_outer)
    g_gram = cross_gram(None, train_grads, 0, place, near + (after(far[2], x_gram),), 0, 2)
    rest = near + (after(far[3], g_gram),)
    return score_shares(x_gram, g_gram, owner_rows, self_terms, train_acts, CUT, place, rest, 2, 2, rest)


def finish(shares, canary_total):
    can = lax.axis_size("can")
    width = CSEQ // can
    total = shares
    for k in range(1, can):
        total = total + lax.ppermute(shares, "can", [(i, (i + k) % can) for i in range(can)])
    own = lax.dynamic_slice(total, (0, lax.axis_index("can") * width), (SEQ_DEV, width))
    scale = math.sqrt(FF * D * (canary_total / CSEQ))
    return own / (scale * jnp.sqrt(total[:SEQ_DEV, CSEQ] / (FF * D) + 1.0)[:, None])


def local(train_acts, train_grads, train_segment, canary_acts, canary_grads, canary_segment):
    tok, can = lax.axis_size("tok"), lax.axis_size("can")
    rows = train_acts.shape[0]
    canary_total = canary_acts.shape[0] * tok * can
    local_ids = train_segment - lax.axis_index("tok") * SEQ_DEV
    owner_rows = (jnp.arange(8, dtype=jnp.int32)[:, None] == local_ids[None, :]).astype(jnp.float32)

    share = rows // can
    start = lax.axis_index("can") * share
    pair = gram(train_acts, lax.dynamic_slice_in_dim(train_acts, start, share, 0))
    pair = pair * gram(train_grads, lax.dynamic_slice_in_dim(train_grads, start, share, 0))
    left = exact(owner_rows, pair, ((1,), (0,)))
    self_terms = left * lax.dynamic_slice_in_dim(owner_rows, start, share, 1)

    if tok == 4:
        shares = line_scores(
            train_acts, train_grads, owner_rows, self_terms, canary_acts, canary_grads, canary_segment
        )
    else:
        ids = lax.all_gather(canary_segment, "tok", axis=0, tiled=True)
        pair = gram(train_acts, lax.all_gather(canary_acts, "tok", axis=0, tiled=True))
        pair = pair * gram(train_grads, lax.all_gather(canary_grads, "tok", axis=0, tiled=True))
        member = (ids[:, None] == jnp.arange(CSEQ, dtype=jnp.int32)[None, :]).astype(jnp.float32)
        scores = exact(exact(owner_rows, pair, ((1,), (0,))), member, ((1,), (0,)))
        self_rows = jnp.broadcast_to(jnp.sum(self_terms, axis=1)[:, None], (8, LANES - CSEQ))
        shares = jnp.concatenate([scores, self_rows], axis=1)
    return finish(shares, canary_total)


def solution(mesh):
    placed = (
        P(("job", "tok"), None),
        P(("job", "tok"), None),
        P(("job", "tok")),
        P(("job", "tok", "can"), None),
        P(("job", "tok", "can"), None),
        P(("job", "tok", "can")),
    )
    return jax.shard_map(
        local, mesh=mesh, in_specs=placed, out_specs=P(("job", "tok"), "can"), check_vma=False
    )
```

```python
import math

import jax
import jax.numpy as jnp
from jax import lax
from jax.experimental import pallas as pl
from jax.experimental.pallas import tpu as pltpu
from jax.sharding import PartitionSpec as P

FF = 14336
D = 4096
SEQ_DEV = 4
CSEQ = 16
LANES = 128
CUT = 10240
SPLIT = 6144
BLOCK = 2048
ROWS = (((1,), (1,)), ((), ()))


def gram(left, right):
    return lax.dot_general(left, right, ROWS, preferred_element_type=jnp.float32)


def exact(left, right, dims):
    return lax.dot_general(
        left, right, (dims, ((), ())), precision=lax.Precision.HIGHEST, preferred_element_type=jnp.float32
    )


def after(value, *earlier):
    return lax.optimization_barrier((value,) + earlier)[0]


def after2(one, two, earlier):
    return lax.optimization_barrier((one, two) + tuple(earlier))[:2]


def call(kernel, inputs, specs, steps, out, scratch, depth, name):
    shapes = out if isinstance(out, list) else [out]
    result = pl.pallas_call(
        kernel,
        grid=(steps,),
        in_specs=specs,
        out_specs=[pl.BlockSpec(shape, lambda k: (0, 0)) for shape in shapes],
        scratch_shapes=scratch,
        out_shape=[jax.ShapeDtypeStruct(shape, jnp.float32) for shape in shapes],
        cost_estimate=pl.CostEstimate(flops=512 * 256 * depth, bytes_accessed=1024 * depth, transcendentals=0),
        compiler_params=pltpu.CompilerParams(vmem_limit_bytes=64 << 20),
        name=name,
    )(*inputs)
    return result if isinstance(out, list) else result[0]


def is_inner():
    z = lax.axis_index("tok")
    return (z == 1) | (z == 2)


def in_order(inner, own, first, middle, middle2, outer, outer2):
    return jnp.concatenate([own, first, jnp.where(inner, middle, outer), jnp.where(inner, middle2, outer2)], axis=0)


def cross_gram(base, train, low, pieces, first, count):
    rows, per = train.shape[0], pieces[0].shape[0]

    def kernel(*refs):
        train_ref, out_ref = refs[-8], refs[-1]
        part = gram(train_ref[...], in_order(is_inner(), *[r[...] for r in refs[-7:-1]]))

        @pl.when(pl.program_id(0) == 0)
        def _():
            out_ref[...] = part if base is None else refs[0][...] + part

        @pl.when(pl.program_id(0) > 0)
        def _():
            out_ref[...] += part

    specs = gram_specs(rows, per, low, first)
    inputs = (train,) + tuple(pieces)
    if base is not None:
        specs = [pl.BlockSpec((rows, 4 * per), lambda k: (0, 0))] + specs
        inputs = (base,) + inputs
    return call(kernel, inputs, specs, count, (rows, 4 * per), [], count * BLOCK, "cross_gram")


def gram_specs(rows, per, low, first):
    near = pl.BlockSpec((per, BLOCK), lambda k: (0, first + k))
    late = pl.BlockSpec((per, BLOCK), lambda k: (0, k))
    return [pl.BlockSpec((rows, BLOCK), lambda k: (0, low // BLOCK + k))] + [near] * 5 + [late]


def score_shares(x_gram, g_gram, owner_rows, self_terms, train, low, pieces, first, tags):
    rows, per = train.shape[0], pieces[0].shape[0]
    count = (train.shape[1] - low) // BLOCK
    can = lax.axis_size("can")
    width = CSEQ // can

    def kernel(x_ref, g_ref, owner_ref, self_ref, *refs):
        inner, total = is_inner(), refs[-1]
        part = gram(refs[0][...], in_order(inner, *[r[...] for r in refs[1:7]]))

        @pl.when(pl.program_id(0) == 0)
        def _():
            total[...] = x_ref[...] + part

        @pl.when(pl.program_id(0) > 0)
        def _():
            total[...] += part

        @pl.when(pl.program_id(0) == count - 1)
        def _():
            by_train = exact(owner_ref[...], total[...] * g_ref[...], ((1,), (0,)))
            ids = in_order(inner, *[r[...].astype(jnp.float32) for r in refs[7:13]])
            lane = lax.broadcasted_iota(jnp.int32, ids.shape, 1)
            scores = exact(by_train, (ids == lane.astype(jnp.float32)).astype(jnp.float32), ((1,), (0,)))
            own = jnp.sum(self_ref[...], axis=1, keepdims=True)
            lane = lax.broadcasted_iota(jnp.int32, scores.shape, 1)
            for k in range(can):
                to = lax.rem(lax.axis_index("can") + k, can)
                shifted = pltpu.roll(scores, lax.rem(LANES - to * width, LANES), 1)
                refs[13 + k][...] = jnp.where(lane < width, shifted, own)

    whole = pl.BlockSpec((rows, 4 * per), lambda k: (0, 0))
    seq = owner_rows.shape[0]
    specs = [
        whole,
        whole,
        pl.BlockSpec((seq, rows), lambda k: (0, 0)),
        pl.BlockSpec(self_terms.shape, lambda k: (0, 0)),
    ]
    specs = specs + gram_specs(rows, per, low, first)
    specs = specs + [pl.BlockSpec((per, LANES), lambda k, at=t.shape[1] // LANES - 1: (0, at)) for t in tags]
    inputs = (x_gram, g_gram, owner_rows, self_terms, train) + tuple(pieces) + tuple(tags)
    scratch = [pltpu.VMEM((rows, 4 * per), jnp.float32)]
    return call(kernel, inputs, specs, count, [(seq, LANES)] * can, scratch, count * BLOCK, "score_shares")


SIDES = [(0, 1), (1, 0), (2, 3), (3, 2)]
MIDDLE = [(1, 2), (2, 1)]
OUTWARD = [(1, 0), (2, 3)]


def line_scores(train_acts, train_grads, owner_rows, self_terms, canary_acts, canary_grads, canary_segment):
    tag = jnp.broadcast_to(canary_segment.astype(canary_grads.dtype)[:, None], (canary_segment.shape[0], LANES))
    x_own = canary_acts[:, :CUT]
    y_own = jnp.concatenate([canary_grads, canary_acts[:, CUT:], tag], axis=1)

    x_first = lax.ppermute(x_own, "tok", SIDES)
    x_middle = lax.ppermute(x_own, "tok", MIDDLE)
    y_first = lax.ppermute(y_own, "tok", SIDES)
    y_middle = lax.ppermute(y_own, "tok", MIDDLE)

    x_first, x_middle = after2(x_first, x_middle, ())
    x_middle2 = lax.ppermute(x_first, "tok", MIDDLE)
    x_outer = lax.ppermute(x_middle, "tok", OUTWARD)
    y_first, y_middle = after2(y_first, y_middle, (x_first, x_middle))
    y_middle2 = lax.ppermute(y_first, "tok", MIDDLE)
    y_outer = lax.ppermute(y_middle, "tok", OUTWARD)

    x_middle2, x_outer = after2(x_middle2, x_outer, (y_first, y_middle))
    part = x_middle2[:, :SPLIT]
    x_far = lax.ppermute(part, "tok", OUTWARD)
    part = after(x_middle2, part)[:, SPLIT:]
    x_far2 = lax.ppermute(part, "tok", OUTWARD)
    y_middle2, y_outer = after2(y_middle2, y_outer, (part, self_terms))
    part = after(y_middle2, y_outer)[:, :D]
    g_far = lax.ppermute(part, "tok", OUTWARD)
    part = after(y_middle2, part)[:, D:]
    y_far = lax.ppermute(part, "tok", OUTWARD)

    near = (x_own, x_first, x_middle, x_middle2, x_outer)
    first = SPLIT // BLOCK
    x_gram = cross_gram(None, train_acts, 0, near + (x_far,), 0, first)
    x_far2 = after(x_far2, x_gram)
    x_gram = cross_gram(x_gram, train_acts, SPLIT, near + (x_far2,), first, CUT // BLOCK - first)
    near = (y_own, y_first, y_middle, y_middle2, y_outer)
    g_gram = cross_gram(None, train_grads, 0, near + (after(g_far, x_gram),), 0, D // BLOCK)
    rest = near + (after(y_far, g_gram),)
    return score_shares(x_gram, g_gram, owner_rows, self_terms, train_acts, CUT, rest, D // BLOCK, rest)


def finish(shares, canary_total):
    can = lax.axis_size("can")
    width = CSEQ // can
    total = shares[0][:SEQ_DEV]
    for k in range(1, can):
        total = total + lax.ppermute(shares[k], "can", [(i, (i + k) % can) for i in range(can)])[:SEQ_DEV]
    scale = math.sqrt(FF * D * (canary_total / CSEQ))
    return total[:, :width] / (scale * jnp.sqrt(total[:, width : 2 * width] / (FF * D) + 1.0))


def local(train_acts, train_grads, train_segment, canary_acts, canary_grads, canary_segment):
    tok, can = lax.axis_size("tok"), lax.axis_size("can")
    rows = train_acts.shape[0]
    canary_total = canary_acts.shape[0] * tok * can
    local_ids = train_segment - lax.axis_index("tok") * SEQ_DEV
    owner_rows = (jnp.arange(8, dtype=jnp.int32)[:, None] == local_ids[None, :]).astype(jnp.float32)

    share = rows // can
    start = lax.axis_index("can") * share
    pair = gram(train_acts, lax.dynamic_slice_in_dim(train_acts, start, share, 0))
    pair = pair * gram(train_grads, lax.dynamic_slice_in_dim(train_grads, start, share, 0))
    left = exact(owner_rows, pair, ((1,), (0,)))
    self_terms = left * lax.dynamic_slice_in_dim(owner_rows, start, share, 1)

    if tok == 4:
        shares = line_scores(
            train_acts, train_grads, owner_rows, self_terms, canary_acts, canary_grads, canary_segment
        )
    else:
        ids = lax.all_gather(canary_segment, "tok", axis=0, tiled=True)
        pair = gram(train_acts, lax.all_gather(canary_acts, "tok", axis=0, tiled=True))
        pair = pair * gram(train_grads, lax.all_gather(canary_grads, "tok", axis=0, tiled=True))
        member = (ids[:, None] == jnp.arange(CSEQ, dtype=jnp.int32)[None, :]).astype(jnp.float32)
        scores = exact(exact(owner_rows, pair, ((1,), (0,))), member, ((1,), (0,)))
        own = jnp.broadcast_to(jnp.sum(self_terms, axis=1)[:, None], (owner_rows.shape[0], CSEQ // can))
        columns = [
            lax.dynamic_slice_in_dim(scores, lax.rem(lax.axis_index("can") + k, can) * (CSEQ // can), CSEQ // can, 1)
            for k in range(can)
        ]
        shares = [jnp.concatenate([c, own], axis=1) for c in columns]
    return finish(shares, canary_total)


def solution(mesh):
    placed = (
        P(("job", "tok"), None),
        P(("job", "tok"), None),
        P(("job", "tok")),
        P(("job", "tok", "can"), None),
        P(("job", "tok", "can"), None),
        P(("job", "tok", "can")),
    )
    return jax.shard_map(
        local, mesh=mesh, in_specs=placed, out_specs=P(("job", "tok"), "can"), check_vma=False
    )
```

```python
import math

import jax
import jax.numpy as jnp
from jax import lax
from jax.experimental import pallas as pl
from jax.experimental.pallas import tpu as pltpu
from jax.sharding import PartitionSpec as P

FF = 14336
D = 4096
SEQ_DEV = 4
CSEQ = 16
LANES = 128
CUT = 10240
SPLIT = 6144
BLOCK = 2048
ROWS = (((1,), (1,)), ((), ()))


def gram(left, right):
    return lax.dot_general(left, right, ROWS, preferred_element_type=jnp.float32)


def exact(left, right, dims):
    return lax.dot_general(
        left, right, (dims, ((), ())), precision=lax.Precision.HIGHEST, preferred_element_type=jnp.float32
    )


def after(value, *earlier):
    return lax.optimization_barrier((value,) + earlier)[0]


def after2(one, two, earlier):
    return lax.optimization_barrier((one, two) + tuple(earlier))[:2]


def call(kernel, inputs, specs, steps, out, scratch, depth, name):
    shapes = out if isinstance(out, list) else [out]
    result = pl.pallas_call(
        kernel,
        grid=(steps,),
        in_specs=specs,
        out_specs=[pl.BlockSpec(shape, lambda k: (0, 0)) for shape in shapes],
        scratch_shapes=scratch,
        out_shape=[jax.ShapeDtypeStruct(shape, jnp.float32) for shape in shapes],
        cost_estimate=pl.CostEstimate(flops=512 * 256 * depth, bytes_accessed=1024 * depth, transcendentals=0),
        compiler_params=pltpu.CompilerParams(vmem_limit_bytes=64 << 20),
        name=name,
    )(*inputs)
    return result if isinstance(out, list) else result[0]


def is_inner():
    z = lax.axis_index("tok")
    return (z == 1) | (z == 2)


def in_order(inner, own, first, middle, middle2, outer, outer2):
    return jnp.concatenate([own, first, jnp.where(inner, middle, outer), jnp.where(inner, middle2, outer2)], axis=0)


def cross_gram(base, train, low, pieces, first, count):
    rows, per = train.shape[0], pieces[0].shape[0]

    def kernel(*refs):
        train_ref, out_ref = refs[-8], refs[-1]
        part = gram(train_ref[...], in_order(is_inner(), *[r[...] for r in refs[-7:-1]]))

        @pl.when(pl.program_id(0) == 0)
        def _():
            out_ref[...] = part if base is None else refs[0][...] + part

        @pl.when(pl.program_id(0) > 0)
        def _():
            out_ref[...] += part

    specs = gram_specs(rows, per, low, first)
    inputs = (train,) + tuple(pieces)
    if base is not None:
        specs = [pl.BlockSpec((rows, 4 * per), lambda k: (0, 0))] + specs
        inputs = (base,) + inputs
    return call(kernel, inputs, specs, count, (rows, 4 * per), [], count * BLOCK, "cross_gram")


def gram_specs(rows, per, low, first):
    near = pl.BlockSpec((per, BLOCK), lambda k: (0, first + k))
    late = pl.BlockSpec((per, BLOCK), lambda k: (0, k))
    return [pl.BlockSpec((rows, BLOCK), lambda k: (0, low // BLOCK + k))] + [near] * 5 + [late]


def score_shares(x_gram, g_gram, owner_rows, self_terms, train, low, pieces, first, tags):
    rows, per = train.shape[0], pieces[0].shape[0]
    count = (train.shape[1] - low) // BLOCK
    can = lax.axis_size("can")
    width = CSEQ // can

    def kernel(x_ref, g_ref, owner_ref, self_ref, *refs):
        inner, total = is_inner(), refs[-1]
        part = gram(refs[0][...], in_order(inner, *[r[...] for r in refs[1:7]]))

        @pl.when(pl.program_id(0) == 0)
        def _():
            total[...] = x_ref[...] + part

        @pl.when(pl.program_id(0) > 0)
        def _():
            total[...] += part

        @pl.when(pl.program_id(0) == count - 1)
        def _():
            by_train = exact(owner_ref[...], total[...] * g_ref[...], ((1,), (0,)))
            ids = in_order(inner, *[r[...].astype(jnp.float32) for r in refs[7:13]])
            lane = lax.broadcasted_iota(jnp.int32, ids.shape, 1)
            scores = exact(by_train, (ids == lane.astype(jnp.float32)).astype(jnp.float32), ((1,), (0,)))
            own = jnp.sum(self_ref[...], axis=1, keepdims=True)
            lane = lax.broadcasted_iota(jnp.int32, scores.shape, 1)
            for k in range(can):
                to = lax.rem(lax.axis_index("can") + k, can)
                shifted = pltpu.roll(scores, lax.rem(LANES - to * width, LANES), 1)
                refs[13 + k][...] = jnp.where(lane < width, shifted, own)

    whole = pl.BlockSpec((rows, 4 * per), lambda k: (0, 0))
    seq = owner_rows.shape[0]
    specs = [
        whole,
        whole,
        pl.BlockSpec((seq, rows), lambda k: (0, 0)),
        pl.BlockSpec(self_terms.shape, lambda k: (0, 0)),
    ]
    specs = specs + gram_specs(rows, per, low, first)
    specs = specs + [pl.BlockSpec((per, LANES), lambda k, at=t.shape[1] // LANES - 1: (0, at)) for t in tags]
    inputs = (x_gram, g_gram, owner_rows, self_terms, train) + tuple(pieces) + tuple(tags)
    scratch = [pltpu.VMEM((rows, 4 * per), jnp.float32)]
    return call(kernel, inputs, specs, count, [(seq, LANES)] * can, scratch, count * BLOCK, "score_shares")


def share_gram(train, share, block):
    def kernel(train_ref, out_ref):
        start = pl.multiple_of(lax.axis_index("can") * share, share)
        part = gram(train_ref[...], train_ref[pl.ds(start, share), :])

        @pl.when(pl.program_id(0) == 0)
        def _():
            out_ref[...] = part

        @pl.when(pl.program_id(0) > 0)
        def _():
            out_ref[...] += part

    rows, depth = train.shape
    specs = [pl.BlockSpec((rows, block), lambda k: (0, k))]
    return call(kernel, (train,), specs, depth // block, (rows, share), [], depth, "share_gram")


SIDES = [(0, 1), (1, 0), (2, 3), (3, 2)]
MIDDLE = [(1, 2), (2, 1)]
OUTWARD = [(1, 0), (2, 3)]


def line_scores(train_acts, train_grads, owner_rows, self_g, self_terms, canary_acts, canary_grads, canary_segment):
    tag = jnp.broadcast_to(canary_segment.astype(canary_grads.dtype)[:, None], (canary_segment.shape[0], LANES))
    x_own = canary_acts[:, :CUT]
    y_own = jnp.concatenate([canary_grads, canary_acts[:, CUT:], tag], axis=1)

    x_first = lax.ppermute(x_own, "tok", SIDES)
    x_middle = lax.ppermute(x_own, "tok", MIDDLE)
    y_first = lax.ppermute(y_own, "tok", SIDES)
    y_middle = lax.ppermute(y_own, "tok", MIDDLE)

    x_first = after(x_first, self_g)
    x_middle = after(x_middle, x_first)
    x_middle2 = lax.ppermute(x_first, "tok", MIDDLE)
    x_outer = lax.ppermute(x_middle, "tok", OUTWARD)
    y_first, y_middle = after2(y_first, y_middle, (x_first, x_middle))
    y_middle2 = lax.ppermute(y_first, "tok", MIDDLE)
    y_outer = lax.ppermute(y_middle, "tok", OUTWARD)

    x_middle2, x_outer = after2(x_middle2, x_outer, (y_first, y_middle, self_terms))
    part = x_middle2[:, :SPLIT]
    x_far = lax.ppermute(part, "tok", OUTWARD)
    part = after(x_middle2, part)[:, SPLIT:]
    x_far2 = lax.ppermute(part, "tok", OUTWARD)
    y_middle2, y_outer = after2(y_middle2, y_outer, (part, self_terms))
    part = after(y_middle2, y_outer)[:, :D]
    g_far = lax.ppermute(part, "tok", OUTWARD)
    part = after(y_middle2, part)[:, D:]
    y_far = lax.ppermute(part, "tok", OUTWARD)

    near = (x_own, x_first, x_middle, x_middle2, x_outer)
    first = SPLIT // BLOCK
    x_gram = cross_gram(None, train_acts, 0, near + (x_far,), 0, first)
    x_far2 = after(x_far2, x_gram)
    x_gram = cross_gram(x_gram, train_acts, SPLIT, near + (x_far2,), first, CUT // BLOCK - first)
    near = (y_own, y_first, y_middle, y_middle2, y_outer)
    g_gram = cross_gram(None, train_grads, 0, near + (after(g_far, x_gram),), 0, D // BLOCK)
    rest = near + (after(y_far, g_gram),)
    return score_shares(x_gram, g_gram, owner_rows, self_terms, train_acts, CUT, rest, D // BLOCK, rest)


def finish(shares, canary_total):
    can = lax.axis_size("can")
    width = CSEQ // can
    total = shares[0][:SEQ_DEV]
    for k in range(1, can):
        total = total + lax.ppermute(shares[k], "can", [(i, (i + k) % can) for i in range(can)])[:SEQ_DEV]
    scale = math.sqrt(FF * D * (canary_total / CSEQ))
    return total[:, :width] / (scale * jnp.sqrt(total[:, width : 2 * width] / (FF * D) + 1.0))


def local(train_acts, train_grads, train_segment, canary_acts, canary_grads, canary_segment):
    tok, can = lax.axis_size("tok"), lax.axis_size("can")
    rows = train_acts.shape[0]
    canary_total = canary_acts.shape[0] * tok * can
    local_ids = train_segment - lax.axis_index("tok") * SEQ_DEV
    owner_rows = (jnp.arange(8, dtype=jnp.int32)[:, None] == local_ids[None, :]).astype(jnp.float32)

    share = rows // can
    start = lax.axis_index("can") * share
    self_g = gram(train_grads, lax.dynamic_slice_in_dim(train_grads, start, share, 0))
    if tok == 4:
        pair = share_gram(train_acts, share, 7 * BLOCK // 4) * self_g
    else:
        pair = gram(train_acts, lax.dynamic_slice_in_dim(train_acts, start, share, 0)) * self_g
    left = exact(owner_rows, pair, ((1,), (0,)))
    self_terms = left * lax.dynamic_slice_in_dim(owner_rows, start, share, 1)

    if tok == 4:
        shares = line_scores(
            train_acts, train_grads, owner_rows, self_g, self_terms, canary_acts, canary_grads, canary_segment
        )
    else:
        ids = lax.all_gather(canary_segment, "tok", axis=0, tiled=True)
        pair = gram(train_acts, lax.all_gather(canary_acts, "tok", axis=0, tiled=True))
        pair = pair * gram(train_grads, lax.all_gather(canary_grads, "tok", axis=0, tiled=True))
        member = (ids[:, None] == jnp.arange(CSEQ, dtype=jnp.int32)[None, :]).astype(jnp.float32)
        scores = exact(exact(owner_rows, pair, ((1,), (0,))), member, ((1,), (0,)))
        own = jnp.broadcast_to(jnp.sum(self_terms, axis=1)[:, None], (owner_rows.shape[0], CSEQ // can))
        columns = [
            lax.dynamic_slice_in_dim(scores, lax.rem(lax.axis_index("can") + k, can) * (CSEQ // can), CSEQ // can, 1)
            for k in range(can)
        ]
        shares = [jnp.concatenate([c, own], axis=1) for c in columns]
    return finish(shares, canary_total)


def solution(mesh):
    placed = (
        P(("job", "tok"), None),
        P(("job", "tok"), None),
        P(("job", "tok")),
        P(("job", "tok", "can"), None),
        P(("job", "tok", "can"), None),
        P(("job", "tok", "can")),
    )
    return jax.shard_map(
        local, mesh=mesh, in_specs=placed, out_specs=P(("job", "tok"), "can"), check_vma=False
    )
```

```python
import math

import jax
import jax.numpy as jnp
from jax import lax
from jax.experimental import pallas as pl
from jax.experimental.pallas import tpu as pltpu
from jax.sharding import PartitionSpec as P

FF = 14336
D = 4096
SEQ_DEV = 4
CSEQ = 16
LANES = 128
CUT = 10240
SPLIT = 6144
BLOCK = 2048
ROWS = (((1,), (1,)), ((), ()))


def gram(left, right):
    return lax.dot_general(left, right, ROWS, preferred_element_type=jnp.float32)


def exact(left, right, dims):
    return lax.dot_general(
        left, right, (dims, ((), ())), precision=lax.Precision.HIGHEST, preferred_element_type=jnp.float32
    )


def after(value, *earlier):
    return lax.optimization_barrier((value,) + earlier)[0]


def after2(one, two, earlier):
    return lax.optimization_barrier((one, two) + tuple(earlier))[:2]


def call(kernel, inputs, specs, steps, out, scratch, depth, name):
    shapes = out if isinstance(out, list) else [out]
    result = pl.pallas_call(
        kernel,
        grid=(steps,),
        in_specs=specs,
        out_specs=[pl.BlockSpec(shape, lambda k: (0, 0)) for shape in shapes],
        scratch_shapes=scratch,
        out_shape=[jax.ShapeDtypeStruct(shape, jnp.float32) for shape in shapes],
        cost_estimate=pl.CostEstimate(flops=512 * 256 * depth, bytes_accessed=1024 * depth, transcendentals=0),
        compiler_params=pltpu.CompilerParams(vmem_limit_bytes=64 << 20),
        name=name,
    )(*inputs)
    return result if isinstance(out, list) else result[0]


def is_inner():
    z = lax.axis_index("tok")
    return (z == 1) | (z == 2)


def in_order(inner, own, first, middle, middle2, outer, outer2):
    return jnp.concatenate([own, first, jnp.where(inner, middle, outer), jnp.where(inner, middle2, outer2)], axis=0)


def cross_gram(base, train, low, pieces, first, count):
    rows, per = train.shape[0], pieces[0].shape[0]

    def kernel(*refs):
        train_ref, out_ref = refs[-8], refs[-1]
        part = gram(train_ref[...], in_order(is_inner(), *[r[...] for r in refs[-7:-1]]))

        @pl.when(pl.program_id(0) == 0)
        def _():
            out_ref[...] = part if base is None else refs[0][...] + part

        @pl.when(pl.program_id(0) > 0)
        def _():
            out_ref[...] += part

    specs = gram_specs(rows, per, low, first)
    inputs = (train,) + tuple(pieces)
    if base is not None:
        specs = [pl.BlockSpec((rows, 4 * per), lambda k: (0, 0))] + specs
        inputs = (base,) + inputs
    return call(kernel, inputs, specs, count, (rows, 4 * per), [], count * BLOCK, "cross_gram")


def gram_specs(rows, per, low, first):
    near = pl.BlockSpec((per, BLOCK), lambda k: (0, first + k))
    late = pl.BlockSpec((per, BLOCK), lambda k: (0, k))
    return [pl.BlockSpec((rows, BLOCK), lambda k: (0, low // BLOCK + k))] + [near] * 5 + [late]


def score_shares(x_gram, g_gram, owner_rows, self_terms, train, low, pieces, first, tags):
    rows, per = train.shape[0], pieces[0].shape[0]
    count = (train.shape[1] - low) // BLOCK
    can = lax.axis_size("can")
    width = CSEQ // can

    def kernel(x_ref, g_ref, owner_ref, self_ref, *refs):
        inner, total = is_inner(), refs[-1]
        part = gram(refs[0][...], in_order(inner, *[r[...] for r in refs[1:7]]))

        @pl.when(pl.program_id(0) == 0)
        def _():
            total[...] = x_ref[...] + part

        @pl.when(pl.program_id(0) > 0)
        def _():
            total[...] += part

        @pl.when(pl.program_id(0) == count - 1)
        def _():
            by_train = exact(owner_ref[...], total[...] * g_ref[...], ((1,), (0,)))
            ids = in_order(inner, *[r[...].astype(jnp.float32) for r in refs[7:13]])
            lane = lax.broadcasted_iota(jnp.int32, ids.shape, 1)
            scores = exact(by_train, (ids == lane.astype(jnp.float32)).astype(jnp.float32), ((1,), (0,)))
            own = jnp.sum(self_ref[...], axis=1, keepdims=True)
            lane = lax.broadcasted_iota(jnp.int32, scores.shape, 1)
            for k in range(can):
                to = lax.rem(lax.axis_index("can") + k, can)
                shifted = pltpu.roll(scores, lax.rem(LANES - to * width, LANES), 1)
                refs[13 + k][...] = jnp.where(lane < width, shifted, own)

    whole = pl.BlockSpec((rows, 4 * per), lambda k: (0, 0))
    seq = owner_rows.shape[0]
    specs = [
        whole,
        whole,
        pl.BlockSpec((seq, rows), lambda k: (0, 0)),
        pl.BlockSpec(self_terms.shape, lambda k: (0, 0)),
    ]
    specs = specs + gram_specs(rows, per, low, first)
    specs = specs + [pl.BlockSpec((per, LANES), lambda k, at=t.shape[1] // LANES - 1: (0, at)) for t in tags]
    inputs = (x_gram, g_gram, owner_rows, self_terms, train) + tuple(pieces) + tuple(tags)
    scratch = [pltpu.VMEM((rows, 4 * per), jnp.float32)]
    return call(kernel, inputs, specs, count, [(seq, LANES)] * can, scratch, count * BLOCK, "score_shares")


def share_gram(train, share, block):
    def kernel(train_ref, out_ref):
        start = pl.multiple_of(lax.axis_index("can") * share, share)
        part = gram(train_ref[...], train_ref[pl.ds(start, share), :])

        @pl.when(pl.program_id(0) == 0)
        def _():
            out_ref[...] = part

        @pl.when(pl.program_id(0) > 0)
        def _():
            out_ref[...] += part

    rows, depth = train.shape
    specs = [pl.BlockSpec((rows, block), lambda k: (0, k))]
    return call(kernel, (train,), specs, depth // block, (rows, share), [], depth, "share_gram")


SIDES = [(0, 1), (1, 0), (2, 3), (3, 2)]
MIDDLE = [(1, 2), (2, 1)]
OUTWARD = [(1, 0), (2, 3)]


def line_scores(train_acts, train_grads, owner_rows, self_g, self_terms, canary_acts, canary_grads, canary_segment):
    tag = jnp.broadcast_to(canary_segment.astype(canary_grads.dtype)[:, None], (canary_segment.shape[0], LANES))
    x_own = canary_acts[:, :CUT]
    y_own = jnp.concatenate([canary_grads, canary_acts[:, CUT:], tag], axis=1)

    x_first = lax.ppermute(x_own, "tok", SIDES)
    x_middle = lax.ppermute(x_own, "tok", MIDDLE)
    y_first = lax.ppermute(y_own, "tok", SIDES)
    y_middle = lax.ppermute(y_own, "tok", MIDDLE)

    x_first = after(x_first, self_g)
    x_middle = after(x_middle, x_first)
    x_middle2 = lax.ppermute(x_first, "tok", MIDDLE)
    x_outer = lax.ppermute(x_middle, "tok", OUTWARD)
    y_first, y_middle = after2(y_first, y_middle, (x_first, x_middle))
    y_middle2 = lax.ppermute(y_first, "tok", MIDDLE)
    y_outer = lax.ppermute(y_middle, "tok", OUTWARD)

    x_middle2, x_outer = after2(x_middle2, x_outer, (y_first, y_middle, self_terms))
    part = x_middle2[:, :SPLIT]
    x_far = lax.ppermute(part, "tok", OUTWARD)
    part = after(x_middle2, part)[:, SPLIT:]
    x_far2 = lax.ppermute(part, "tok", OUTWARD)
    y_middle2, y_outer = after2(y_middle2, y_outer, (part, self_terms))
    part = after(y_middle2, y_outer)[:, :D]
    g_far = lax.ppermute(part, "tok", OUTWARD)
    part = after(y_middle2, part)[:, D:]
    y_far = lax.ppermute(part, "tok", OUTWARD)

    near = (x_own, x_first, x_middle, x_middle2, x_outer)
    first = SPLIT // BLOCK
    x_gram = cross_gram(None, train_acts, 0, near + (x_far,), 0, first)
    x_far2 = after(x_far2, x_gram)
    x_gram = cross_gram(x_gram, train_acts, SPLIT, near + (x_far2,), first, CUT // BLOCK - first)
    near = (y_own, y_first, y_middle, y_middle2, y_outer)
    g_gram = cross_gram(None, train_grads, 0, near + (after(g_far, x_gram),), 0, D // BLOCK)
    rest = near + (after(y_far, g_gram),)
    return score_shares(x_gram, g_gram, owner_rows, self_terms, train_acts, CUT, rest, D // BLOCK, rest)


def finish(shares, canary_total):
    can = lax.axis_size("can")
    width = CSEQ // can
    total = lax.optimization_barrier(shares[0][:SEQ_DEV])
    for k in range(1, can):
        total = total + lax.ppermute(shares[k], "can", [(i, (i + k) % can) for i in range(can)])[:SEQ_DEV]
    scale = math.sqrt(FF * D * (canary_total / CSEQ))
    return total[:, :width] / (scale * jnp.sqrt(total[:, width : 2 * width] / (FF * D) + 1.0))


def local(train_acts, train_grads, train_segment, canary_acts, canary_grads, canary_segment):
    tok, can = lax.axis_size("tok"), lax.axis_size("can")
    rows = train_acts.shape[0]
    canary_total = canary_acts.shape[0] * tok * can
    local_ids = train_segment - lax.axis_index("tok") * SEQ_DEV
    owner_rows = (jnp.arange(8, dtype=jnp.int32)[:, None] == local_ids[None, :]).astype(jnp.float32)

    share = rows // can
    start = lax.axis_index("can") * share
    self_g = gram(train_grads, lax.dynamic_slice_in_dim(train_grads, start, share, 0))
    if tok == 4:
        pair = share_gram(train_acts, share, 7 * BLOCK // 4) * self_g
    else:
        pair = gram(train_acts, lax.dynamic_slice_in_dim(train_acts, start, share, 0)) * self_g
    left = exact(owner_rows, pair, ((1,), (0,)))
    self_terms = left * lax.dynamic_slice_in_dim(owner_rows, start, share, 1)

    if tok == 4:
        shares = line_scores(
            train_acts, train_grads, owner_rows, self_g, self_terms, canary_acts, canary_grads, canary_segment
        )
    else:
        ids = lax.all_gather(canary_segment, "tok", axis=0, tiled=True)
        pair = gram(train_acts, lax.all_gather(canary_acts, "tok", axis=0, tiled=True))
        pair = pair * gram(train_grads, lax.all_gather(canary_grads, "tok", axis=0, tiled=True))
        member = (ids[:, None] == jnp.arange(CSEQ, dtype=jnp.int32)[None, :]).astype(jnp.float32)
        scores = exact(exact(owner_rows, pair, ((1,), (0,))), member, ((1,), (0,)))
        own = jnp.broadcast_to(jnp.sum(self_terms, axis=1)[:, None], (owner_rows.shape[0], CSEQ // can))
        columns = [
            lax.dynamic_slice_in_dim(scores, lax.rem(lax.axis_index("can") + k, can) * (CSEQ // can), CSEQ // can, 1)
            for k in range(can)
        ]
        shares = [jnp.concatenate([c, own], axis=1) for c in columns]
    return finish(shares, canary_total)


def solution(mesh):
    placed = (
        P(("job", "tok"), None),
        P(("job", "tok"), None),
        P(("job", "tok")),
        P(("job", "tok", "can"), None),
        P(("job", "tok", "can"), None),
        P(("job", "tok", "can")),
    )
    return jax.shard_map(
        local, mesh=mesh, in_specs=placed, out_specs=P(("job", "tok"), "can"), check_vma=False
    )
```

```python
import math

import jax
import jax.numpy as jnp
from jax import lax
from jax.experimental import pallas as pl
from jax.experimental.pallas import tpu as pltpu
from jax.sharding import PartitionSpec as P

FF = 14336
D = 4096
SEQ_DEV = 4
CSEQ = 16
LANES = 128
CUT = 10240
SPLIT = 6144
BLOCK = 2048
ROWS = (((1,), (1,)), ((), ()))


def gram(left, right):
    return lax.dot_general(left, right, ROWS, preferred_element_type=jnp.float32)


def exact(left, right, dims):
    return lax.dot_general(
        left, right, (dims, ((), ())), precision=lax.Precision.HIGHEST, preferred_element_type=jnp.float32
    )


def after(value, *earlier):
    return lax.optimization_barrier((value,) + earlier)[0]


def after2(one, two, earlier):
    return lax.optimization_barrier((one, two) + tuple(earlier))[:2]


def call(kernel, inputs, specs, steps, out, scratch, depth, name):
    shapes = out if isinstance(out, list) else [out]
    result = pl.pallas_call(
        kernel,
        grid=(steps,),
        in_specs=specs,
        out_specs=[pl.BlockSpec(shape, lambda k: (0, 0)) for shape in shapes],
        scratch_shapes=scratch,
        out_shape=[jax.ShapeDtypeStruct(shape, jnp.float32) for shape in shapes],
        cost_estimate=pl.CostEstimate(flops=512 * 256 * depth, bytes_accessed=1024 * depth, transcendentals=0),
        compiler_params=pltpu.CompilerParams(vmem_limit_bytes=64 << 20),
        name=name,
    )(*inputs)
    return result if isinstance(out, list) else result[0]


def is_inner():
    z = lax.axis_index("tok")
    return (z == 1) | (z == 2)


def in_order(inner, own, first, middle, middle2, outer, outer2):
    return jnp.concatenate([own, first, jnp.where(inner, middle, outer), jnp.where(inner, middle2, outer2)], axis=0)


def cross_gram(base, train, low, pieces, first, count):
    rows, per = train.shape[0], pieces[0].shape[0]

    def kernel(*refs):
        train_ref, out_ref = refs[-8], refs[-1]
        part = gram(train_ref[...], in_order(is_inner(), *[r[...] for r in refs[-7:-1]]))

        @pl.when(pl.program_id(0) == 0)
        def _():
            out_ref[...] = part if base is None else refs[0][...] + part

        @pl.when(pl.program_id(0) > 0)
        def _():
            out_ref[...] += part

    specs = gram_specs(rows, per, low, first)
    inputs = (train,) + tuple(pieces)
    if base is not None:
        specs = [pl.BlockSpec((rows, 4 * per), lambda k: (0, 0))] + specs
        inputs = (base,) + inputs
    return call(kernel, inputs, specs, count, (rows, 4 * per), [], count * BLOCK, "cross_gram")


def gram_specs(rows, per, low, first):
    near = pl.BlockSpec((per, BLOCK), lambda k: (0, first + k))
    late = pl.BlockSpec((per, BLOCK), lambda k: (0, k))
    return [pl.BlockSpec((rows, BLOCK), lambda k: (0, low // BLOCK + k))] + [near] * 5 + [late]


def score_shares(x_gram, g_gram, owner_rows, self_terms, train, low, pieces, first, tags):
    rows, per = train.shape[0], pieces[0].shape[0]
    count = (train.shape[1] - low) // BLOCK
    can = lax.axis_size("can")
    width = CSEQ // can

    def kernel(x_ref, g_ref, owner_ref, self_ref, *refs):
        inner, total = is_inner(), refs[-1]
        part = gram(refs[0][...], in_order(inner, *[r[...] for r in refs[1:7]]))

        @pl.when(pl.program_id(0) == 0)
        def _():
            total[...] = x_ref[...] + part

        @pl.when(pl.program_id(0) > 0)
        def _():
            total[...] += part

        @pl.when(pl.program_id(0) == count - 1)
        def _():
            by_train = exact(owner_ref[...], total[...] * g_ref[...], ((1,), (0,)))
            ids = in_order(inner, *[r[...].astype(jnp.float32) for r in refs[7:13]])
            lane = lax.broadcasted_iota(jnp.int32, ids.shape, 1)
            scores = exact(by_train, (ids == lane.astype(jnp.float32)).astype(jnp.float32), ((1,), (0,)))
            own = jnp.sum(self_ref[...], axis=1, keepdims=True)
            lane = lax.broadcasted_iota(jnp.int32, scores.shape, 1)
            for k in range(can):
                to = lax.axis_index("can") ^ k
                shifted = pltpu.roll(scores, lax.rem(LANES - to * width, LANES), 1)
                refs[13 + k][...] = jnp.where(lane < width, shifted, own)

    whole = pl.BlockSpec((rows, 4 * per), lambda k: (0, 0))
    seq = owner_rows.shape[0]
    specs = [
        whole,
        whole,
        pl.BlockSpec((seq, rows), lambda k: (0, 0)),
        pl.BlockSpec(self_terms.shape, lambda k: (0, 0)),
    ]
    specs = specs + gram_specs(rows, per, low, first)
    specs = specs + [pl.BlockSpec((per, LANES), lambda k, at=t.shape[1] // LANES - 1: (0, at)) for t in tags]
    inputs = (x_gram, g_gram, owner_rows, self_terms, train) + tuple(pieces) + tuple(tags)
    scratch = [pltpu.VMEM((rows, 4 * per), jnp.float32)]
    return call(kernel, inputs, specs, count, [(seq, LANES)] * can, scratch, count * BLOCK, "score_shares")


def share_gram(train, share, block):
    def kernel(train_ref, out_ref):
        start = pl.multiple_of(lax.axis_index("can") * share, share)
        part = gram(train_ref[...], train_ref[pl.ds(start, share), :])

        @pl.when(pl.program_id(0) == 0)
        def _():
            out_ref[...] = part

        @pl.when(pl.program_id(0) > 0)
        def _():
            out_ref[...] += part

    rows, depth = train.shape
    specs = [pl.BlockSpec((rows, block), lambda k: (0, k))]
    return call(kernel, (train,), specs, depth // block, (rows, share), [], depth, "share_gram")


SIDES = [(0, 1), (1, 0), (2, 3), (3, 2)]
MIDDLE = [(1, 2), (2, 1)]
OUTWARD = [(1, 0), (2, 3)]


def line_scores(train_acts, train_grads, owner_rows, self_g, self_terms, canary_acts, canary_grads, canary_segment):
    tag = jnp.broadcast_to(canary_segment.astype(canary_grads.dtype)[:, None], (canary_segment.shape[0], LANES))
    x_own = canary_acts[:, :CUT]
    y_own = jnp.concatenate([canary_grads, canary_acts[:, CUT:], tag], axis=1)

    x_first = lax.ppermute(x_own, "tok", SIDES)
    x_middle = lax.ppermute(x_own, "tok", MIDDLE)
    y_first = lax.ppermute(y_own, "tok", SIDES)
    y_middle = lax.ppermute(y_own, "tok", MIDDLE)

    x_first = after(x_first, self_g)
    x_middle = after(x_middle, x_first)
    x_middle2 = lax.ppermute(x_first, "tok", MIDDLE)
    x_outer = lax.ppermute(x_middle, "tok", OUTWARD)
    y_first, y_middle = after2(y_first, y_middle, (x_first, x_middle))
    y_middle2 = lax.ppermute(y_first, "tok", MIDDLE)
    y_outer = lax.ppermute(y_middle, "tok", OUTWARD)

    x_middle2, x_outer = after2(x_middle2, x_outer, (y_first, y_middle, self_terms))
    part = x_middle2[:, :SPLIT]
    x_far = lax.ppermute(part, "tok", OUTWARD)
    part = after(x_middle2, part)[:, SPLIT:]
    x_far2 = lax.ppermute(part, "tok", OUTWARD)
    y_middle2, y_outer = after2(y_middle2, y_outer, (part, self_terms))
    part = after(y_middle2, y_outer)[:, :D]
    g_far = lax.ppermute(part, "tok", OUTWARD)
    part = after(y_middle2, part)[:, D:]
    y_far = lax.ppermute(part, "tok", OUTWARD)

    near = (x_own, x_first, x_middle, x_middle2, x_outer)
    first = SPLIT // BLOCK
    x_gram = cross_gram(None, train_acts, 0, near + (x_far,), 0, first)
    x_far2 = after(x_far2, x_gram)
    x_gram = cross_gram(x_gram, train_acts, SPLIT, near + (x_far2,), first, CUT // BLOCK - first)
    near = (y_own, y_first, y_middle, y_middle2, y_outer)
    g_gram = cross_gram(None, train_grads, 0, near + (after(g_far, x_gram),), 0, D // BLOCK)
    rest = near + (after(y_far, g_gram),)
    return score_shares(x_gram, g_gram, owner_rows, self_terms, train_acts, CUT, rest, D // BLOCK, rest)


def finish(shares, canary_total):
    can = lax.axis_size("can")
    width = CSEQ // can
    total = lax.optimization_barrier(shares[0][:SEQ_DEV])
    for k in range(1, can):
        total = total + lax.ppermute(shares[k], "can", [(i, i ^ k) for i in range(can)])[:SEQ_DEV]
    scale = math.sqrt(FF * D * (canary_total / CSEQ))
    return total[:, :width] / (scale * jnp.sqrt(total[:, width : 2 * width] / (FF * D) + 1.0))


def local(train_acts, train_grads, train_segment, canary_acts, canary_grads, canary_segment):
    tok, can = lax.axis_size("tok"), lax.axis_size("can")
    rows = train_acts.shape[0]
    canary_total = canary_acts.shape[0] * tok * can
    local_ids = train_segment - lax.axis_index("tok") * SEQ_DEV
    owner_rows = (jnp.arange(8, dtype=jnp.int32)[:, None] == local_ids[None, :]).astype(jnp.float32)

    share = rows // can
    start = lax.axis_index("can") * share
    self_g = gram(train_grads, lax.dynamic_slice_in_dim(train_grads, start, share, 0))
    if tok == 4:
        pair = share_gram(train_acts, share, 7 * BLOCK // 4) * self_g
    else:
        pair = gram(train_acts, lax.dynamic_slice_in_dim(train_acts, start, share, 0)) * self_g
    left = exact(owner_rows, pair, ((1,), (0,)))
    self_terms = left * lax.dynamic_slice_in_dim(owner_rows, start, share, 1)

    if tok == 4:
        shares = line_scores(
            train_acts, train_grads, owner_rows, self_g, self_terms, canary_acts, canary_grads, canary_segment
        )
    else:
        ids = lax.all_gather(canary_segment, "tok", axis=0, tiled=True)
        pair = gram(train_acts, lax.all_gather(canary_acts, "tok", axis=0, tiled=True))
        pair = pair * gram(train_grads, lax.all_gather(canary_grads, "tok", axis=0, tiled=True))
        member = (ids[:, None] == jnp.arange(CSEQ, dtype=jnp.int32)[None, :]).astype(jnp.float32)
        scores = exact(exact(owner_rows, pair, ((1,), (0,))), member, ((1,), (0,)))
        own = jnp.broadcast_to(jnp.sum(self_terms, axis=1)[:, None], (owner_rows.shape[0], CSEQ // can))
        columns = [
            lax.dynamic_slice_in_dim(scores, (lax.axis_index("can") ^ k) * (CSEQ // can), CSEQ // can, 1)
            for k in range(can)
        ]
        shares = [jnp.concatenate([c, own], axis=1) for c in columns]
    return finish(shares, canary_total)


def solution(mesh):
    placed = (
        P(("job", "tok"), None),
        P(("job", "tok"), None),
        P(("job", "tok")),
        P(("job", "tok", "can"), None),
        P(("job", "tok", "can"), None),
        P(("job", "tok", "can")),
    )
    return jax.shard_map(
        local, mesh=mesh, in_specs=placed, out_specs=P(("job", "tok"), "can"), check_vma=False
    )
```
